1024 devices in a mesh: gx: 32 (over y, x), gy: 4 (over z_hi), gz: 8 (over z_lo, core).
Axes of the slice: x: 4, y: 8, z: 16 (z_hi: 4, z_lo: 4; z = z_hi * 4 + z_lo), core: 2. Of those that a mesh axis runs over, the one named last changes fastest.
Arguments:
- amplitudes: float32 [5, 256, 12288], P(None, 'gz', ('gx', 'gy')), may hold values from -24 to 24
- integrals: float32 [5, 12288, 12288], P(None, 'gx', ('gy', 'gz')), may hold values from -0.0546875 to 0.0546875
- pair_counts: int32 [5], replicated, may hold values from 1 to 12288, 57600 in all
- row_counts: int32 [5], replicated, may hold values from 1 to 256, 1000 in all
Outputs:
- cycle_residual: float32 [5, 256, 12288], P(None, 'gx', ('gy', 'gz'))
The draws below stay inside these ranges and needn't reach their ends.
Inputs may be any that keep to these rules, and one draw needn't show every extreme that they name: `pair_counts`: used pair slots of each block; they sum to 57600 and some block uses all 12288. `row_counts`: used row slots of each block; they sum to 1000 and some block uses all 256.
All inputs are finite; a program needn't handle non-finite values.
Results may differ from the reference program's by a relative error of at most 0.0003.
Values sent between devices are 32-bit elements; how exact they have to be, the bound alone decides.
No kernel may reach another device: no remote copies, remote signals or barrier semaphores. Data moves between devices by JAX's collectives and lax.ppermute only.
A program may use at most 32 MiB of HBM per device.

```python
import math
import jax
import jax.numpy as jnp
import numpy as np
from jax import lax

BLOCKS = 5
CAP = 12288
ROWCAP = 256
PAIR_TOTAL = 57600
ROW_TOTAL = 1000


def strengthened(values, own_key, source, target, parts, factor):
    owner, partner = [(jnp.arange(values.shape[dim]) // (values.shape[dim] // parts)).reshape([-1 if axis == dim else 1 for axis in range(values.ndim)]) for dim in (source, target)]
    chosen = jax.random.permutation(own_key, parts)[partner]
    strong = (owner == chosen) | (owner == (partner + parts // 2) % parts)
    return jnp.where(strong, factor * values, values)


def levels(key, dims, cuts, low, high):
    gain, own = 1.0, jax.random.fold_in(key, 6)
    for position, shards_of in cuts:
        heights = jnp.exp(jax.random.uniform(jax.random.fold_in(own, position), (shards_of,), jnp.float32, low / len(cuts), high / len(cuts)))
        gain = gain * jnp.repeat(heights, dims[position] // shards_of).reshape([-1 if axis == position else 1 for axis in range(len(dims))])
    return gain


def profile(count, total, limit, slope):
    weights = [(1 << 20) // math.isqrt(standing ** slope) + 1 for standing in range(2, count + 1)]
    surplus, counts = total - limit - (count - 1), [1] * (count - 1)
    while surplus > 0:
        free = [i for i in range(count - 1) if counts[i] < limit]
        pool, left = sum([weights[i] for i in free]), surplus
        for i in free:
            more = min(limit - counts[i], max(1, left * weights[i] // pool), surplus)
            counts[i] = counts[i] + more
            surplus = surplus - more
    return np.array([limit] + counts)


def ragged(key, count, total, limit, slope):
    if count == 2:
        one = jax.random.randint(key, (), max(1, total - limit), min(limit, total - 1) + 1)
        return jnp.stack([one, total - one])
    sizes = jnp.asarray(profile(count, total, limit, slope), jnp.int32)
    pairs = (count - 1) // 2
    donor, taker = sizes[1:1 + 2 * pairs:2], sizes[2:2 + 2 * pairs:2]
    room = jnp.minimum(donor - 1, limit - taker)
    passed = jax.random.randint(jax.random.fold_in(key, 1), (pairs,), 0, 1 << 20) % (room + 1)
    sizes = sizes.at[1:1 + 2 * pairs:2].set(donor - passed).at[2:2 + 2 * pairs:2].set(taker + passed)
    return sizes[jax.random.permutation(jax.random.fold_in(key, 2), count)]


def bell_draw(key, extent, deviation, limit, split=(), dtype=jnp.bfloat16):
    entries = jax.random.normal(key, extent, jnp.float32) * deviation
    if len(split) > 0:
        entries = levels(key, extent, split, -0.22, 0.18) * entries
    return jnp.clip(entries, min=-limit, max=limit).astype(dtype)


def heavy_noise(rng, shape, deviation, bound, shards, heavy, kind=jnp.bfloat16):
    drawn = deviation * jax.random.normal(rng, shape, jnp.float32)
    if shards:
        drawn = drawn * levels(rng, shape, shards, -0.22, 0.18)
    return jnp.clip(strengthened(drawn, jax.random.fold_in(rng, 3), *heavy), -bound, bound).astype(kind)


def setup_inputs(seed: int = 0) -> dict:
    key_of = jax.random.split(jax.random.key(seed), 5)
    amplitudes = heavy_noise(key_of[0], (BLOCKS, ROWCAP, CAP), 1.0, 24.0, ((1, 8), (2, 128)), (2, 1, 128, 5.5), jnp.float32)
    integrals = bell_draw(key_of[1], (BLOCKS, CAP, CAP), CAP ** -0.5, 0.0546875, ((1, 32), (2, 32)), jnp.float32)
    pair_counts = ragged(key_of[2], BLOCKS, PAIR_TOTAL, CAP, 1).astype(jnp.int32)
    row_counts = ragged(key_of[3], BLOCKS, ROW_TOTAL, ROWCAP, 1).astype(jnp.int32)
    return dict(amplitudes=amplitudes, integrals=integrals, pair_counts=pair_counts, row_counts=row_counts)


def reference(amplitudes, integrals, pair_counts, row_counts):
    slots = lax.iota(jnp.int32, CAP)
    rows = lax.iota(jnp.int32, ROWCAP)

    def one_block(items):
        amp, integ, pair_count, row_count = items
        keep = jnp.logical_and(rows[:, None] < row_count, slots[None, :] < pair_count)
        masked = jnp.where(keep, amp, jnp.zeros_like(amp))
        result = jnp.dot(masked, integ, precision=lax.Precision.HIGHEST, preferred_element_type=jnp.float32)
        return jnp.where(slots[None, :] < pair_count, result, jnp.zeros_like(result))

    return lax.map(one_block, (amplitudes, integrals, pair_counts, row_counts))
```

```python
import functools

import jax
import jax.numpy as jnp
from jax import lax
from jax.experimental import pallas as pl
from jax.experimental.pallas import tpu as pltpu
from jax.sharding import Mesh
from jax.sharding import PartitionSpec as P

NX, NY, ZH, ZL, CORES = 4, 8, 4, 4, 2
BLOCKS, ROWS, PAIRS, COLS = 5, 32, 96, 384
LANES = 128


def product(counts_ref, where_ref, own_ref, other_ref, integrals_ref, out_ref, ahi, alo, bhi, blo):
    g = pl.program_id(0)

    @pl.when(g == 0)
    def _():
        for ref in (ahi, alo, bhi, blo):
            ref[...] = jnp.zeros_like(ref)

    core = where_ref[0]
    left = counts_ref[g] - where_ref[1]
    half = ZL * ROWS
    lane = lax.broadcasted_iota(jnp.int32, (half, PAIRS), 1)
    for h in range(ZH):
        keep = lane + h * PAIRS < left
        for part, ref in enumerate((own_ref, other_ref)):
            a = ref[h * ZL:(h + 1) * ZL, 0].reshape(half, PAIRS)
            a = jnp.where(keep, a, 0.0)
            high = a.astype(jnp.bfloat16)
            low = (a - high.astype(jnp.float32)).astype(jnp.bfloat16)
            ahi[part * half:(part + 1) * half, h * LANES:h * LANES + PAIRS] = high
            alo[part * half:(part + 1) * half, h * LANES:h * LANES + PAIRS] = low
        b = integrals_ref[0, h * PAIRS:(h + 1) * PAIRS, :]
        high = b.astype(jnp.bfloat16)
        bhi[h * LANES:h * LANES + PAIRS, :] = high
        blo[h * LANES:h * LANES + PAIRS, :] = (b - high.astype(jnp.float32)).astype(jnp.bfloat16)
    dot = functools.partial(jnp.dot, preferred_element_type=jnp.float32)
    total = dot(ahi[...], bhi[...]) + (dot(ahi[...], blo[...]) + dot(alo[...], bhi[...]))
    for part in range(CORES):
        side = core if part == 0 else 1 - core
        for l in range(ZL):
            for x in range(NX):
                first = part * half + l * ROWS + x * 8
                out_ref[x, 2 * l + side, 0] = total[first:first + 8]


def per_device(amplitudes, integrals, pair_counts, row_counts):
    gx = lax.axis_index("y") * NX + lax.axis_index("x")
    core = lax.axis_index("c")
    own = lax.all_gather(amplitudes, ("zh", "zl"), axis=0, tiled=False)
    other = lax.ppermute(own, "c", [(0, 1), (1, 0)])
    where = jnp.stack([core, gx * COLS]).astype(jnp.int32)
    slab = pl.BlockSpec((ZH * ZL, 1, ROWS, PAIRS), lambda g, *_: (0, g, 0, 0))
    partial = pl.pallas_call(
        product,
        out_shape=jax.ShapeDtypeStruct((NX, NY, BLOCKS, 8, COLS), jnp.float32),
        grid_spec=pltpu.PrefetchScalarGridSpec(
            num_scalar_prefetch=2,
            grid=(BLOCKS,),
            in_specs=[slab, slab, pl.BlockSpec((1, COLS, COLS), lambda g, *_: (g, 0, 0))],
            out_specs=pl.BlockSpec((NX, NY, 1, 8, COLS), lambda g, *_: (0, 0, g, 0, 0)),
            scratch_shapes=[pltpu.VMEM((CORES * ZL * ROWS, ZH * LANES), jnp.bfloat16)] * 2
            + [pltpu.VMEM((ZH * LANES, COLS), jnp.bfloat16)] * 2,
        ),
        compiler_params=pltpu.CompilerParams(vmem_limit_bytes=24 * 1024 * 1024),
        cost_estimate=pl.CostEstimate(flops=1_200_000_000, bytes_accessed=8_000_000, transcendentals=0),
    )(pair_counts, where, own, other, integrals)
    along_x = lax.all_to_all(partial, "x", 0, 0, tiled=True).sum(0)
    along_y = lax.all_to_all(along_x, "y", 0, 0, tiled=True).sum(0)
    column_first = (lax.axis_index("zh") * ZL * CORES + lax.axis_index("zl") * CORES + core) * COLS
    column_used = column_first + lax.iota(jnp.int32, COLS)[None, :] < pair_counts[:, None]
    row_used = gx * 8 + lax.iota(jnp.int32, 8)[None, :] < row_counts[:, None]
    keep = jnp.logical_and(row_used[:, :, None], column_used[:, None, :])
    return jnp.where(keep, along_y, 0.0)


def solution(mesh):
    fine = Mesh(mesh.devices.reshape(NY, NX, ZH, ZL, CORES), ("y", "x", "zh", "zl", "c"))
    out = P(None, ("y", "x"), ("zh", "zl", "c"))
    return jax.shard_map(
        per_device,
        mesh=fine,
        in_specs=(P(None, ("zl", "c"), ("y", "x", "zh")), out, P(), P()),
        out_specs=out,
        check_vma=False,
    )
```

```python
import functools

import jax
import jax.numpy as jnp
from jax import lax
from jax.experimental import pallas as pl
from jax.experimental.pallas import tpu as pltpu
from jax.sharding import Mesh
from jax.sharding import PartitionSpec as P

NX, YH, YL, ZH, ZL, CORES = 4, 4, 2, 4, 4, 2
BLOCKS, ROWS, PAIRS, COLS = 5, 32, 96, 384
LANES = 128
HALF = ZL * ROWS


def product(meta_ref, slab_ref, integrals_ref, *rest):
    out_ref, ahi, alo, bhi, blo, held, arrived = rest[-7:]
    g = pl.program_id(0)

    def fetch(block):
        return pltpu.make_async_copy(integrals_ref.at[block], held.at[block], arrived.at[block])

    @pl.when(g == 0)
    def _():
        for block in range(BLOCKS):
            fetch(block).start()
        for ref in (ahi, alo, bhi, blo):
            ref[...] = jnp.zeros_like(ref)

    left = meta_ref[g]
    lane = lax.broadcasted_iota(jnp.int32, (HALF, PAIRS), 1)
    for h in range(ZH):
        a = slab_ref[h * ZL:(h + 1) * ZL, 0].reshape(HALF, PAIRS)
        a = jnp.where(lane + h * PAIRS < left, a, 0.0)
        high = a.astype(jnp.bfloat16)
        ahi[:, h * LANES:h * LANES + PAIRS] = high
        alo[:, h * LANES:h * LANES + PAIRS] = (a - high.astype(jnp.float32)).astype(jnp.bfloat16)
    fetch(g).wait()
    for h in range(ZH):
        b = held[g, h * PAIRS:(h + 1) * PAIRS, :]
        high = b.astype(jnp.bfloat16)
        bhi[h * LANES:h * LANES + PAIRS, :] = high
        blo[h * LANES:h * LANES + PAIRS, :] = (b - high.astype(jnp.float32)).astype(jnp.bfloat16)
    dot = functools.partial(jnp.dot, preferred_element_type=jnp.float32)
    total = dot(ahi[...], bhi[...]) + (dot(ahi[...], blo[...]) + dot(alo[...], bhi[...]))
    for l in range(ZL):
        for x in range(NX):
            first = l * ROWS + x * 8
            out_ref[0, x, l, 0] = total[first:first + 8]


def partial_sums(meta, slab, integrals, filled=None):
    extra = [] if filled is None else [filled]
    return pl.pallas_call(
        product,
        out_shape=jax.ShapeDtypeStruct((YL, NX, YH, BLOCKS, 8, COLS), jnp.float32),
        grid_spec=pltpu.PrefetchScalarGridSpec(
            num_scalar_prefetch=1,
            grid=(BLOCKS,),
            in_specs=[
                pl.BlockSpec((ZH * ZL, 1, ROWS, PAIRS), lambda g, *_: (0, g, 0, 0)),
                pl.BlockSpec(memory_space=pltpu.HBM),
            ] + [pl.BlockSpec(memory_space=pl.ANY)] * len(extra),
            out_specs=pl.BlockSpec(
                (1, NX, YH, 1, 8, COLS), lambda g, meta: (meta[BLOCKS], 0, 0, g, 0, 0)
            ),
            scratch_shapes=[pltpu.VMEM((HALF, ZH * LANES), jnp.bfloat16)] * 2
            + [pltpu.VMEM((ZH * LANES, COLS), jnp.bfloat16)] * 2
            + [pltpu.VMEM((BLOCKS, COLS, COLS), jnp.float32), pltpu.SemaphoreType.DMA((BLOCKS,))],
        ),
        input_output_aliases={3: 0} if extra else {},
        compiler_params=pltpu.CompilerParams(vmem_limit_bytes=54_000_000),
        cost_estimate=pl.CostEstimate(flops=600_000_000, bytes_accessed=6_000_000, transcendentals=0),
    )(meta, slab, integrals, *extra)


def per_device(amplitudes, integrals, pair_counts, row_counts):
    y = lax.axis_index("yh") * YL + lax.axis_index("yl")
    gx = y * NX + lax.axis_index("x")
    core = lax.axis_index("c")
    own = lax.all_gather(amplitudes, ("zh", "zl"), axis=0, tiled=False)
    other = lax.ppermute(own, "c", [(0, 1), (1, 0)])
    left = pair_counts - gx * COLS
    filled = partial_sums(jnp.append(left, core), own, integrals)
    partial = partial_sums(jnp.append(left, 1 - core), other, integrals, filled)
    sent = partial.reshape(YL * NX, YH * BLOCKS * 8, COLS)
    near = lax.all_to_all(sent, ("yl", "x"), 0, 0, tiled=True).sum(0)
    far = lax.all_to_all(near.reshape(YH, BLOCKS * 8, COLS), "yh", 0, 0, tiled=True).sum(0)
    column_first = ((lax.axis_index("zh") * ZL + lax.axis_index("zl")) * CORES + core) * COLS
    column_used = column_first + lax.iota(jnp.int32, COLS)[None, :] < pair_counts[:, None]
    row_used = gx * 8 + lax.iota(jnp.int32, 8)[None, :] < row_counts[:, None]
    keep = jnp.logical_and(row_used[:, :, None], column_used[:, None, :])
    return jnp.where(keep, far.reshape(BLOCKS, 8, COLS), 0.0)


def solution(mesh):
    fine = Mesh(
        mesh.devices.reshape(YH, YL, NX, ZH, ZL, CORES), ("yh", "yl", "x", "zh", "zl", "c")
    )
    out = P(None, ("yh", "yl", "x"), ("zh", "zl", "c"))
    return jax.shard_map(
        per_device,
        mesh=fine,
        in_specs=(P(None, ("zl", "c"), ("yh", "yl", "x", "zh")), out, P(), P()),
        out_specs=out,
        check_vma=False,
    )
```

```python
import functools

import jax
import jax.numpy as jnp
from jax import lax
from jax.experimental import pallas as pl
from jax.experimental.pallas import tpu as pltpu
from jax.sharding import Mesh
from jax.sharding import PartitionSpec as P

NX, NY, ZH, ZL, CORES = 4, 8, 4, 4, 2
BLOCKS, ROWS, PAIRS, COLS = 5, 32, 96, 384
LANES = 128
HALF = ZL * ROWS
FULL = CORES * HALF


def product(meta_ref, own_ref, other_ref, integrals_ref, *rest):
    outs, (a2, bhi, blo, total, held, arrived) = rest[:NX], rest[NX:]
    g = pl.program_id(0)

    def fetch(block):
        return pltpu.make_async_copy(integrals_ref.at[block], held.at[block], arrived.at[block])

    @pl.when(g == 0)
    def _():
        for block in range(BLOCKS):
            fetch(block).start()
        for ref in (a2, bhi, blo):
            ref[...] = jnp.zeros_like(ref)

    left, core, me = meta_ref[g], meta_ref[BLOCKS], meta_ref[BLOCKS + 1]
    lane = lax.broadcasted_iota(jnp.int32, (HALF, PAIRS), 1)
    for h in range(ZH):
        keep = lane + h * PAIRS < left
        at = slice(h * LANES, h * LANES + PAIRS)
        for part, ref in enumerate((own_ref, other_ref)):
            a = ref[h * ZL:(h + 1) * ZL, 0].reshape(HALF, PAIRS)
            a = jnp.where(keep, a, 0.0)
            high = a.astype(jnp.bfloat16)
            low = (a - high.astype(jnp.float32)).astype(jnp.bfloat16)
            a2[part * HALF:(part + 1) * HALF, at] = high
            a2[FULL + part * HALF:FULL + (part + 1) * HALF, at] = low
    fetch(g).wait()
    for h in range(ZH):
        b = held[g, h * PAIRS:(h + 1) * PAIRS, :]
        high = b.astype(jnp.bfloat16)
        bhi[h * LANES:h * LANES + PAIRS, :] = high
        blo[h * LANES:h * LANES + PAIRS, :] = (b - high.astype(jnp.float32)).astype(jnp.bfloat16)
    dot = functools.partial(jnp.dot, preferred_element_type=jnp.float32)
    both = dot(a2[...], bhi[...])
    total[...] = both[:FULL] + (both[FULL:] + dot(a2[:FULL], blo[...]))
    for step, out_ref in enumerate(outs):
        x = lax.rem(me + step, NX)
        for part in range(CORES):
            side = core if part == 0 else 1 - core
            for l in range(ZL):
                first = pl.multiple_of(part * HALF + l * ROWS + x * 8, 8)
                out_ref[2 * l + side, 0] = total[pl.ds(first, 8), :]


def partial_sums(meta, own, other, integrals):
    slab = pl.BlockSpec((ZH * ZL, 1, ROWS, PAIRS), lambda g, *_: (0, g, 0, 0))
    return pl.pallas_call(
        product,
        out_shape=[jax.ShapeDtypeStruct((NY, BLOCKS, 8, COLS), jnp.float32)] * NX,
        grid_spec=pltpu.PrefetchScalarGridSpec(
            num_scalar_prefetch=1,
            grid=(BLOCKS,),
            in_specs=[slab, slab, pl.BlockSpec(memory_space=pltpu.HBM)],
            out_specs=[pl.BlockSpec((NY, 1, 8, COLS), lambda g, *_: (0, g, 0, 0))] * NX,
            scratch_shapes=[
                pltpu.VMEM((2 * FULL, ZH * LANES), jnp.bfloat16),
                pltpu.VMEM((ZH * LANES, COLS), jnp.bfloat16),
                pltpu.VMEM((ZH * LANES, COLS), jnp.bfloat16),
                pltpu.VMEM((FULL, COLS), jnp.float32),
                pltpu.VMEM((BLOCKS, COLS, COLS), jnp.float32),
                pltpu.SemaphoreType.DMA((BLOCKS,)),
            ],
        ),
        compiler_params=pltpu.CompilerParams(vmem_limit_bytes=50_500_000),
        cost_estimate=pl.CostEstimate(flops=1_200_000_000, bytes_accessed=8_000_000, transcendentals=0),
    )(meta, own, other, integrals)


def per_device(amplitudes, integrals, pair_counts, row_counts):
    x = lax.axis_index("x")
    gx = lax.axis_index("y") * NX + x
    core = lax.axis_index("c")
    own = lax.all_gather(amplitudes, ("zh", "zl"), axis=0, tiled=False)
    other = lax.ppermute(own, "c", [(0, 1), (1, 0)])
    meta = jnp.concatenate([pair_counts - gx * COLS, jnp.stack([core, x])])
    near, *away = partial_sums(meta, own, other, integrals)
    for step in (2, 1, 3):
        ring = [(i, (i + step) % NX) for i in range(NX)]
        near = near + lax.ppermute(away[step - 1], "x", ring)
    far = lax.all_to_all(near.reshape(NY, BLOCKS * 8, COLS), "y", 0, 0, tiled=True).sum(0)
    column_first = ((lax.axis_index("zh") * ZL + lax.axis_index("zl")) * CORES + core) * COLS
    column_used = column_first + lax.iota(jnp.int32, COLS)[None, :] < pair_counts[:, None]
    row_used = gx * 8 + lax.iota(jnp.int32, 8)[None, :] < row_counts[:, None]
    keep = jnp.logical_and(row_used[:, :, None], column_used[:, None, :])
    return jnp.where(keep, far.reshape(BLOCKS, 8, COLS), 0.0)


def solution(mesh):
    fine = Mesh(mesh.devices.reshape(NY, NX, ZH, ZL, CORES), ("y", "x", "zh", "zl", "c"))
    out = P(None, ("y", "x"), ("zh", "zl", "c"))
    return jax.shard_map(
        per_device,
        mesh=fine,
        in_specs=(P(None, ("zl", "c"), ("y", "x", "zh")), out, P(), P()),
        out_specs=out,
        check_vma=False,
    )
```

```python
import functools

import jax
import jax.numpy as jnp
from jax import lax
from jax.experimental import pallas as pl
from jax.experimental.pallas import tpu as pltpu
from jax.sharding import Mesh
from jax.sharding import PartitionSpec as P

NX, YH, YL, ZH, ZL, CORES = 4, 4, 2, 4, 4, 2
BLOCKS, ROWS, PAIRS, COLS = 5, 32, 96, 384
LANES = 128
HALF = ZL * ROWS
FULL = CORES * HALF
LIMIT = 24 * 1024 * 1024


def split(integrals_ref, bhi_ref, blo_ref):
    pad = jnp.zeros((LANES - PAIRS, COLS), jnp.bfloat16)
    for h in range(ZH):
        b = integrals_ref[0, h * PAIRS:(h + 1) * PAIRS, :]
        high = b.astype(jnp.bfloat16)
        low = (b - high.astype(jnp.float32)).astype(jnp.bfloat16)
        for ref, value in ((bhi_ref, high), (blo_ref, low)):
            ref[0, h * LANES:h * LANES + PAIRS, :] = value
            ref[0, h * LANES + PAIRS:(h + 1) * LANES, :] = pad


def split_integrals(integrals):
    halves = pl.BlockSpec((1, ZH * LANES, COLS), lambda g: (g, 0, 0))
    return pl.pallas_call(
        split,
        out_shape=[jax.ShapeDtypeStruct((BLOCKS, ZH * LANES, COLS), jnp.bfloat16)] * 2,
        grid=(BLOCKS,),
        in_specs=[pl.BlockSpec((1, COLS, COLS), lambda g: (g, 0, 0))],
        out_specs=[halves, halves],
        compiler_params=pltpu.CompilerParams(vmem_limit_bytes=LIMIT),
        cost_estimate=pl.CostEstimate(flops=5_000_000, bytes_accessed=7_000_000, transcendentals=0),
    )(integrals)


def product(meta_ref, own_ref, other_ref, bhi_ref, blo_ref, out_ref, ahi, alo):
    for h in range(ZH):
        pad = slice(h * LANES + PAIRS, (h + 1) * LANES)
        for ref in (ahi, alo):
            ref[:, :, pad] = jnp.zeros((2, FULL, LANES - PAIRS), jnp.bfloat16)

    core = meta_ref[BLOCKS]
    lane = lax.broadcasted_iota(jnp.int32, (HALF, PAIRS), 1)
    dot = functools.partial(jnp.dot, preferred_element_type=jnp.float32)
    for g in range(BLOCKS):
        slot = g % 2
        left = meta_ref[g]
        for h in range(ZH):
            keep = lane < left - h * PAIRS
            at = slice(h * LANES, h * LANES + PAIRS)
            for part, ref in enumerate((own_ref, other_ref)):
                rows = slice(part * HALF, (part + 1) * HALF)
                a = ref[h * ZL:(h + 1) * ZL, g].reshape(HALF, PAIRS)
                a = jnp.where(keep, a, 0.0)
                high = a.astype(jnp.bfloat16)
                ahi[slot, rows, at] = high
                alo[slot, rows, at] = (a - high.astype(jnp.float32)).astype(jnp.bfloat16)
        total = dot(ahi[slot], bhi_ref[g]) + (dot(ahi[slot], blo_ref[g]) + dot(alo[slot], bhi_ref[g]))
        for part in range(CORES):
            side = core if part == 0 else 1 - core
            for l in range(ZL):
                for x in range(NX):
                    first = part * HALF + l * ROWS + x * 8
                    out_ref[side, x, l, g] = total[first:first + 8]


def partial_sums(meta, own, other, integrals):
    whole = pl.BlockSpec(memory_space=pltpu.VMEM)
    bhi, blo = split_integrals(integrals)
    return pl.pallas_call(
        product,
        out_shape=jax.ShapeDtypeStruct((YL, NX, YH, BLOCKS, 8, COLS), jnp.float32),
        in_specs=[pl.BlockSpec(memory_space=pltpu.SMEM)] + [whole] * 4,
        out_specs=whole,
        scratch_shapes=[pltpu.VMEM((2, FULL, ZH * LANES), jnp.bfloat16)] * 2,
        compiler_params=pltpu.CompilerParams(vmem_limit_bytes=LIMIT),
        cost_estimate=pl.CostEstimate(flops=1_200_000_000, bytes_accessed=8_000_000, transcendentals=0),
    )(meta, own, other, bhi, blo)


def per_device(amplitudes, integrals, pair_counts, row_counts):
    y = lax.axis_index("yh") * YL + lax.axis_index("yl")
    gx = y * NX + lax.axis_index("x")
    core = lax.axis_index("c")
    own = lax.all_gather(amplitudes, ("zh", "zl"), axis=0, tiled=False)
    other = lax.ppermute(own, "c", [(0, 1), (1, 0)])
    partial = partial_sums(jnp.append(pair_counts - gx * COLS, core), own, other, integrals)
    sent = partial.reshape(YL * NX, YH * BLOCKS * 8, COLS)
    near = lax.all_to_all(sent, ("yl", "x"), 0, 0, tiled=True).sum(0)
    far = lax.all_to_all(near.reshape(YH, BLOCKS * 8, COLS), "yh", 0, 0, tiled=True).sum(0)
    column_first = ((lax.axis_index("zh") * ZL + lax.axis_index("zl")) * CORES + core) * COLS
    column_used = column_first + lax.iota(jnp.int32, COLS)[None, :] < pair_counts[:, None]
    row_used = gx * 8 + lax.iota(jnp.int32, 8)[None, :] < row_counts[:, None]
    keep = jnp.logical_and(row_used[:, :, None], column_used[:, None, :])
    return jnp.where(keep, far.reshape(BLOCKS, 8, COLS), 0.0)


def solution(mesh):
    fine = Mesh(
        mesh.devices.reshape(YH, YL, NX, ZH, ZL, CORES), ("yh", "yl", "x", "zh", "zl", "c")
    )
    out = P(None, ("yh", "yl", "x"), ("zh", "zl", "c"))
    return jax.shard_map(
        per_device,
        mesh=fine,
        in_specs=(P(None, ("zl", "c"), ("yh", "yl", "x", "zh")), out, P(), P()),
        out_specs=out,
        check_vma=False,
    )
```

```python
import functools

import jax
import jax.numpy as jnp
from jax import lax
from jax.experimental import pallas as pl
from jax.experimental.pallas import tpu as pltpu
from jax.sharding import Mesh
from jax.sharding import PartitionSpec as P

NX, YH, YL, ZH, ZL, CORES = 4, 4, 2, 4, 4, 2
BLOCKS, ROWS, PAIRS, COLS = 5, 32, 96, 384
LANES = 128
PACKED = ROWS * PAIRS // LANES
HALF = ZL * ROWS
FULL = CORES * HALF
LIMIT = 24 * 1024 * 1024


def split(integrals_ref, bhi_ref, blo_ref):
    pad = jnp.zeros((LANES - PAIRS, COLS), jnp.bfloat16)
    for h in range(ZH):
        b = integrals_ref[0, h * PAIRS:(h + 1) * PAIRS, :]
        high = b.astype(jnp.bfloat16)
        low = (b - high.astype(jnp.float32)).astype(jnp.bfloat16)
        for ref, value in ((bhi_ref, high), (blo_ref, low)):
            ref[0, h * LANES:h * LANES + PAIRS, :] = value
            ref[0, h * LANES + PAIRS:(h + 1) * LANES, :] = pad


def split_integrals(integrals):
    halves = pl.BlockSpec((1, ZH * LANES, COLS), lambda g: (g, 0, 0))
    return pl.pallas_call(
        split,
        out_shape=[jax.ShapeDtypeStruct((BLOCKS, ZH * LANES, COLS), jnp.bfloat16)] * 2,
        grid=(BLOCKS,),
        in_specs=[pl.BlockSpec((1, COLS, COLS), lambda g: (g, 0, 0))],
        out_specs=[halves, halves],
        compiler_params=pltpu.CompilerParams(vmem_limit_bytes=LIMIT),
        cost_estimate=pl.CostEstimate(flops=5_000_000, bytes_accessed=7_000_000, transcendentals=0),
    )(integrals)


def pack(amplitudes):
    third = LANES - PAIRS
    last = [amplitudes[:, PACKED:, i * third:(i + 1) * third] for i in range(3)]
    return jnp.concatenate([amplitudes[:, :PACKED], jnp.concatenate(last, axis=1)], axis=2)


def unpack(rows):
    last = [rows[:, i * 8:(i + 1) * 8, PAIRS:] for i in range(3)]
    return jnp.concatenate([rows[:, :, :PAIRS], jnp.concatenate(last, axis=2)], axis=1)


def product(meta_ref, own_ref, other_ref, bhi_ref, blo_ref, out_ref, ahi, alo, result, sent):
    core = meta_ref[BLOCKS]

    def send(g, part):
        side = core if part == 0 else 1 - core
        return pltpu.make_async_copy(result.at[g, part], out_ref.at[side, :, :, g], sent.at[g, part])

    for h in range(ZH):
        pad = slice(h * LANES + PAIRS, (h + 1) * LANES)
        for ref in (ahi, alo):
            ref[:, :, pad] = jnp.zeros((2, FULL, LANES - PAIRS), jnp.bfloat16)

    lane = lax.broadcasted_iota(jnp.int32, (HALF, PAIRS), 1)
    dot = functools.partial(jnp.dot, preferred_element_type=jnp.float32)
    for g in range(BLOCKS):
        slot = g % 2
        left = meta_ref[g]
        for h in range(ZH):
            keep = lane < left - h * PAIRS
            at = slice(h * LANES, h * LANES + PAIRS)
            for part, ref in enumerate((own_ref, other_ref)):
                rows = slice(part * HALF, (part + 1) * HALF)
                a = unpack(ref[h * ZL:(h + 1) * ZL, g]).reshape(HALF, PAIRS)
                a = jnp.where(keep, a, 0.0)
                high = a.astype(jnp.bfloat16)
                ahi[slot, rows, at] = high
                alo[slot, rows, at] = (a - high.astype(jnp.float32)).astype(jnp.bfloat16)
        total = dot(ahi[slot], bhi_ref[g]) + (dot(ahi[slot], blo_ref[g]) + dot(alo[slot], bhi_ref[g]))
        for part in range(CORES):
            for l in range(ZL):
                for x in range(NX):
                    first = part * HALF + l * ROWS + x * 8
                    result[g, part, x, l] = total[first:first + 8]
            send(g, part).start()
    for g in range(BLOCKS):
        for part in range(CORES):
            send(g, part).wait()


def partial_sums(meta, own, other, integrals):
    whole = pl.BlockSpec(memory_space=pltpu.VMEM)
    bhi, blo = split_integrals(integrals)
    return pl.pallas_call(
        product,
        out_shape=jax.ShapeDtypeStruct((YL, NX, YH, BLOCKS, 8, COLS), jnp.float32),
        in_specs=[pl.BlockSpec(memory_space=pltpu.SMEM)] + [whole] * 4,
        out_specs=pl.BlockSpec(memory_space=pltpu.HBM),
        scratch_shapes=[pltpu.VMEM((2, FULL, ZH * LANES), jnp.bfloat16)] * 2
        + [
            pltpu.VMEM((BLOCKS, CORES, NX, YH, 8, COLS), jnp.float32),
            pltpu.SemaphoreType.DMA((BLOCKS, CORES)),
        ],
        compiler_params=pltpu.CompilerParams(vmem_limit_bytes=LIMIT),
        cost_estimate=pl.CostEstimate(flops=1_200_000_000, bytes_accessed=8_000_000, transcendentals=0),
    )(meta, own, other, bhi, blo)


def per_device(amplitudes, integrals, pair_counts, row_counts):
    y = lax.axis_index("yh") * YL + lax.axis_index("yl")
    gx = y * NX + lax.axis_index("x")
    core = lax.axis_index("c")
    own = lax.all_gather(pack(amplitudes), ("zh", "zl"), axis=0, tiled=False)
    other = lax.ppermute(own, "c", [(0, 1), (1, 0)])
    partial = partial_sums(jnp.append(pair_counts - gx * COLS, core), own, other, integrals)
    sent = partial.reshape(YL * NX, YH * BLOCKS * 8, COLS)
    near = lax.all_to_all(sent, ("yl", "x"), 0, 0, tiled=True).sum(0)
    far = lax.all_to_all(near.reshape(YH, BLOCKS * 8, COLS), "yh", 0, 0, tiled=True).sum(0)
    column_first = ((lax.axis_index("zh") * ZL + lax.axis_index("zl")) * CORES + core) * COLS
    column_used = column_first + lax.iota(jnp.int32, COLS)[None, :] < pair_counts[:, None]
    row_used = gx * 8 + lax.iota(jnp.int32, 8)[None, :] < row_counts[:, None]
    keep = jnp.logical_and(row_used[:, :, None], column_used[:, None, :])
    return jnp.where(keep, far.reshape(BLOCKS, 8, COLS), 0.0)


def solution(mesh):
    fine = Mesh(
        mesh.devices.reshape(YH, YL, NX, ZH, ZL, CORES), ("yh", "yl", "x", "zh", "zl", "c")
    )
    out = P(None, ("yh", "yl", "x"), ("zh", "zl", "c"))
    return jax.shard_map(
        per_device,
        mesh=fine,
        in_specs=(P(None, ("zl", "c"), ("yh", "yl", "x", "zh")), out, P(), P()),
        out_specs=out,
        check_vma=False,
    )
```

```python
import functools

import jax
import jax.numpy as jnp
from jax import lax
from jax.experimental import pallas as pl
from jax.experimental.pallas import tpu as pltpu
from jax.sharding import Mesh
from jax.sharding import PartitionSpec as P

NX, YH, YL, ZH, ZL, CORES = 4, 4, 2, 4, 4, 2
BLOCKS, ROWS, PAIRS, COLS = 5, 32, 96, 384
LANES = 128
PACKED = ROWS * PAIRS // LANES
HALF = ZL * ROWS
FULL = CORES * HALF
LIMIT = 24 * 1024 * 1024
COLUMN_LEFT, ROW_LEFT = BLOCKS + 1, 2 * BLOCKS + 1


def split(integrals_ref, bhi_ref, blo_ref):
    pad = jnp.zeros((LANES - PAIRS, COLS), jnp.bfloat16)
    for h in range(ZH):
        b = integrals_ref[0, h * PAIRS:(h + 1) * PAIRS, :]
        high = b.astype(jnp.bfloat16)
        low = (b - high.astype(jnp.float32)).astype(jnp.bfloat16)
        for ref, value in ((bhi_ref, high), (blo_ref, low)):
            ref[0, h * LANES:h * LANES + PAIRS, :] = value
            ref[0, h * LANES + PAIRS:(h + 1) * LANES, :] = pad


def split_integrals(integrals):
    halves = pl.BlockSpec((1, ZH * LANES, COLS), lambda g: (g, 0, 0))
    return pl.pallas_call(
        split,
        out_shape=[jax.ShapeDtypeStruct((BLOCKS, ZH * LANES, COLS), jnp.bfloat16)] * 2,
        grid=(BLOCKS,),
        in_specs=[pl.BlockSpec((1, COLS, COLS), lambda g: (g, 0, 0))],
        out_specs=[halves, halves],
        compiler_params=pltpu.CompilerParams(vmem_limit_bytes=LIMIT),
        cost_estimate=pl.CostEstimate(flops=5_000_000, bytes_accessed=7_000_000, transcendentals=0),
    )(integrals)


def pack(rows_ref, packed_ref):
    third = LANES - PAIRS
    rows = rows_ref[...]
    last = [rows[:, PACKED:, i * third:(i + 1) * third] for i in range(3)]
    packed_ref[:, :, :PAIRS] = rows[:, :PACKED]
    packed_ref[:, :, PAIRS:] = jnp.concatenate(last, axis=1)


def pack_rows(amplitudes):
    whole = pl.BlockSpec(memory_space=pltpu.VMEM)
    return pl.pallas_call(
        pack,
        out_shape=jax.ShapeDtypeStruct((BLOCKS, PACKED, LANES), jnp.float32),
        in_specs=[whole],
        out_specs=whole,
        compiler_params=pltpu.CompilerParams(vmem_limit_bytes=LIMIT),
    )(amplitudes)


def unpack(rows):
    last = [rows[:, i * 8:(i + 1) * 8, PAIRS:] for i in range(3)]
    return jnp.concatenate([rows[:, :, :PAIRS], jnp.concatenate(last, axis=2)], axis=1)


def product(meta_ref, own_ref, other_ref, bhi_ref, blo_ref, out_ref, ahi, alo):
    core = meta_ref[BLOCKS]

    for h in range(ZH):
        pad = slice(h * LANES + PAIRS, (h + 1) * LANES)
        for ref in (ahi, alo):
            ref[:, :, pad] = jnp.zeros((2, FULL, LANES - PAIRS), jnp.bfloat16)

    lane = lax.broadcasted_iota(jnp.int32, (HALF, PAIRS), 1)
    dot = functools.partial(jnp.dot, preferred_element_type=jnp.float32)
    for g in range(BLOCKS):
        slot = g % 2
        left = meta_ref[g]
        for h in range(ZH):
            keep = lane < left - h * PAIRS
            at = slice(h * LANES, h * LANES + PAIRS)
            for part, ref in enumerate((own_ref, other_ref)):
                rows = slice(part * HALF, (part + 1) * HALF)
                a = unpack(ref[h * ZL:(h + 1) * ZL, g]).reshape(HALF, PAIRS)
                a = jnp.where(keep, a, 0.0)
                high = a.astype(jnp.bfloat16)
                ahi[slot, rows, at] = high
                alo[slot, rows, at] = (a - high.astype(jnp.float32)).astype(jnp.bfloat16)
        total = dot(ahi[slot], bhi_ref[g]) + (dot(ahi[slot], blo_ref[g]) + dot(alo[slot], bhi_ref[g]))
        for part in range(CORES):
            side = core if part == 0 else 1 - core
            for l in range(ZL):
                for x in range(NX):
                    first = part * HALF + l * ROWS + x * 8
                    out_ref[side, x, l, g] = total[first:first + 8]


def partial_sums(meta, own, other, integrals):
    whole = pl.BlockSpec(memory_space=pltpu.VMEM)
    bhi, blo = split_integrals(integrals)
    return pl.pallas_call(
        product,
        out_shape=jax.ShapeDtypeStruct((YL, NX, YH, BLOCKS, 8, COLS), jnp.float32),
        in_specs=[pl.BlockSpec(memory_space=pltpu.SMEM)] + [whole] * 4,
        out_specs=whole,
        scratch_shapes=[pltpu.VMEM((2, FULL, ZH * LANES), jnp.bfloat16)] * 2,
        compiler_params=pltpu.CompilerParams(vmem_limit_bytes=LIMIT),
        cost_estimate=pl.CostEstimate(flops=1_200_000_000, bytes_accessed=8_000_000, transcendentals=0),
    )(meta, own, other, bhi, blo)


def finish(meta_ref, parts_ref, out_ref):
    row = lax.broadcasted_iota(jnp.int32, (8, COLS), 0)
    column = lax.broadcasted_iota(jnp.int32, (8, COLS), 1)
    for g in range(BLOCKS):
        rows = slice(g * 8, (g + 1) * 8)
        total = (parts_ref[0, rows] + parts_ref[1, rows]) + (parts_ref[2, rows] + parts_ref[3, rows])
        used = jnp.logical_and(row < meta_ref[ROW_LEFT + g], column < meta_ref[COLUMN_LEFT + g])
        out_ref[g] = jnp.where(used, total, 0.0)


def final_rows(meta, parts):
    whole = pl.BlockSpec(memory_space=pltpu.VMEM)
    return pl.pallas_call(
        finish,
        out_shape=jax.ShapeDtypeStruct((BLOCKS, 8, COLS), jnp.float32),
        in_specs=[pl.BlockSpec(memory_space=pltpu.SMEM), whole],
        out_specs=whole,
        compiler_params=pltpu.CompilerParams(vmem_limit_bytes=LIMIT),
    )(meta, parts)


def per_device(amplitudes, integrals, pair_counts, row_counts):
    y = lax.axis_index("yh") * YL + lax.axis_index("yl")
    gx = y * NX + lax.axis_index("x")
    core = lax.axis_index("c")
    column_first = ((lax.axis_index("zh") * ZL + lax.axis_index("zl")) * CORES + core) * COLS
    meta = jnp.concatenate(
        [pair_counts - gx * COLS, core[None], pair_counts - column_first, row_counts - gx * 8]
    )
    own = lax.all_gather(pack_rows(amplitudes), ("zh", "zl"), axis=0, tiled=False)
    other = lax.ppermute(own, "c", [(0, 1), (1, 0)])
    partial = partial_sums(meta, own, other, integrals)
    sent = partial.reshape(YL * NX, YH * BLOCKS * 8, COLS)
    near = lax.all_to_all(sent, ("yl", "x"), 0, 0, tiled=True).sum(0)
    far = lax.all_to_all(near.reshape(YH, BLOCKS * 8, COLS), "yh", 0, 0, tiled=True)
    return final_rows(meta, far)


def solution(mesh):
    fine = Mesh(
        mesh.devices.reshape(YH, YL, NX, ZH, ZL, CORES), ("yh", "yl", "x", "zh", "zl", "c")
    )
    out = P(None, ("yh", "yl", "x"), ("zh", "zl", "c"))
    return jax.shard_map(
        per_device,
        mesh=fine,
        in_specs=(P(None, ("zl", "c"), ("yh", "yl", "x", "zh")), out, P(), P()),
        out_specs=out,
        check_vma=False,
    )
```

```python
import functools

import jax
import jax.numpy as jnp
from jax import lax
from jax.experimental import pallas as pl
from jax.experimental.pallas import tpu as pltpu
from jax.sharding import Mesh
from jax.sharding import PartitionSpec as P

NX, YH, YL, ZH, ZL, CORES = 4, 4, 2, 4, 4, 2
BLOCKS, ROWS, PAIRS, COLS = 5, 32, 96, 384
LANES = 128
PACKED = ROWS * PAIRS // LANES
HALF = ZL * ROWS
FULL = CORES * HALF
LIMIT = 24 * 1024 * 1024
COLUMN_LEFT, ROW_LEFT = BLOCKS + 1, 2 * BLOCKS + 1


def split(integrals_ref, bhi_ref, blo_ref):
    pad = jnp.zeros((LANES - PAIRS, COLS), jnp.bfloat16)
    for h in range(ZH):
        b = integrals_ref[0, h * PAIRS:(h + 1) * PAIRS, :]
        high = b.astype(jnp.bfloat16)
        low = (b - high.astype(jnp.float32)).astype(jnp.bfloat16)
        for ref, value in ((bhi_ref, high), (blo_ref, low)):
            ref[0, h * LANES:h * LANES + PAIRS, :] = value
            ref[0, h * LANES + PAIRS:(h + 1) * LANES, :] = pad


def split_integrals(integrals):
    halves = pl.BlockSpec((1, ZH * LANES, COLS), lambda g: (g, 0, 0))
    return pl.pallas_call(
        split,
        out_shape=[jax.ShapeDtypeStruct((BLOCKS, ZH * LANES, COLS), jnp.bfloat16)] * 2,
        grid=(BLOCKS,),
        in_specs=[pl.BlockSpec((1, COLS, COLS), lambda g: (g, 0, 0))],
        out_specs=[halves, halves],
        compiler_params=pltpu.CompilerParams(vmem_limit_bytes=LIMIT),
        cost_estimate=pl.CostEstimate(flops=5_000_000, bytes_accessed=7_000_000, transcendentals=0),
    )(integrals)


def pack(rows_ref, packed_ref):
    third = LANES - PAIRS
    rows = rows_ref[...]
    last = [rows[:, PACKED:, i * third:(i + 1) * third] for i in range(3)]
    packed_ref[:, :, :PAIRS] = rows[:, :PACKED]
    packed_ref[:, :, PAIRS:] = jnp.concatenate(last, axis=1)


def pack_rows(amplitudes):
    whole = pl.BlockSpec(memory_space=pltpu.VMEM)
    return pl.pallas_call(
        pack,
        out_shape=jax.ShapeDtypeStruct((BLOCKS, PACKED, LANES), jnp.float32),
        in_specs=[whole],
        out_specs=whole,
        compiler_params=pltpu.CompilerParams(vmem_limit_bytes=LIMIT),
    )(amplitudes)


def unpack(rows):
    last = [rows[:, i * 8:(i + 1) * 8, PAIRS:] for i in range(3)]
    return jnp.concatenate([rows[:, :, :PAIRS], jnp.concatenate(last, axis=2)], axis=1)


def product(meta_ref, own_ref, other_ref, bhi_ref, blo_ref, out_ref, ahi, alo):
    group = meta_ref[BLOCKS]
    for h in range(ZH):
        pad = slice(h * LANES + PAIRS, (h + 1) * LANES)
        for ref in (ahi, alo):
            ref[:, :, pad] = jnp.zeros((2, FULL, LANES - PAIRS), jnp.bfloat16)

    lane = lax.broadcasted_iota(jnp.int32, (HALF, PAIRS), 1)
    dot = functools.partial(jnp.dot, preferred_element_type=jnp.float32)
    for g in range(BLOCKS):
        slot = g % 2
        left = meta_ref[g]
        for h in range(ZH):
            keep = lane < left - h * PAIRS
            at = slice(h * LANES, h * LANES + PAIRS)
            for part, ref in enumerate((own_ref, other_ref)):
                rows = slice(part * HALF, (part + 1) * HALF)
                a = unpack(ref[h * ZL:(h + 1) * ZL, g]).reshape(HALF, PAIRS)
                a = jnp.where(keep, a, 0.0)
                high = a.astype(jnp.bfloat16)
                ahi[slot, rows, at] = high
                alo[slot, rows, at] = (a - high.astype(jnp.float32)).astype(jnp.bfloat16)
        total = dot(ahi[slot], bhi_ref[g]) + (dot(ahi[slot], blo_ref[g]) + dot(alo[slot], bhi_ref[g]))
        for part in range(CORES):
            for l in range(ZL):
                side = group if (l + part) % 2 == 0 else 1 - group
                for x in range(NX):
                    first = part * HALF + l * ROWS + x * 8
                    out_ref[side, x, l, g] = total[first:first + 8]


def partial_sums(meta, own, other, integrals):
    whole = pl.BlockSpec(memory_space=pltpu.VMEM)
    bhi, blo = split_integrals(integrals)
    return pl.pallas_call(
        product,
        out_shape=jax.ShapeDtypeStruct((YL, NX, YH, BLOCKS, 8, COLS), jnp.float32),
        in_specs=[pl.BlockSpec(memory_space=pltpu.SMEM)] + [whole] * 4,
        out_specs=whole,
        scratch_shapes=[pltpu.VMEM((2, FULL, ZH * LANES), jnp.bfloat16)] * 2,
        compiler_params=pltpu.CompilerParams(vmem_limit_bytes=LIMIT),
        cost_estimate=pl.CostEstimate(flops=1_200_000_000, bytes_accessed=8_000_000, transcendentals=0),
    )(meta, own, other, bhi, blo)


def finish(meta_ref, parts_ref, out_ref):
    row = lax.broadcasted_iota(jnp.int32, (8, COLS), 0)
    column = lax.broadcasted_iota(jnp.int32, (8, COLS), 1)
    for g in range(BLOCKS):
        rows = slice(g * 8, (g + 1) * 8)
        total = (parts_ref[0, rows] + parts_ref[1, rows]) + (parts_ref[2, rows] + parts_ref[3, rows])
        used = jnp.logical_and(row < meta_ref[ROW_LEFT + g], column < meta_ref[COLUMN_LEFT + g])
        out_ref[g] = jnp.where(used, total, 0.0)


def final_rows(meta, parts):
    whole = pl.BlockSpec(memory_space=pltpu.VMEM)
    return pl.pallas_call(
        finish,
        out_shape=jax.ShapeDtypeStruct((BLOCKS, 8, COLS), jnp.float32),
        in_specs=[pl.BlockSpec(memory_space=pltpu.SMEM), whole],
        out_specs=whole,
        compiler_params=pltpu.CompilerParams(vmem_limit_bytes=LIMIT),
    )(meta, parts)


def per_device(amplitudes, integrals, pair_counts, row_counts):
    y = lax.axis_index("yh") * YL + lax.axis_index("yl")
    gx = y * NX + lax.axis_index("x")
    core = lax.axis_index("c")
    group = lax.rem(core + lax.axis_index("zl"), CORES)
    column_first = ((lax.axis_index("zh") * ZL + lax.axis_index("zl")) * CORES + core) * COLS
    meta = jnp.concatenate(
        [pair_counts - gx * COLS, group[None], pair_counts - column_first, row_counts - gx * 8]
    )
    rings = [[z * CORES + (q + z) % CORES for z in range(ZH * ZL)] for q in range(CORES)]
    own = lax.all_gather(pack_rows(amplitudes), ("zh", "zl", "c"), axis_index_groups=rings)
    other = lax.ppermute(own, "c", [(0, 1), (1, 0)])
    partial = partial_sums(meta, own, other, integrals)
    sent = partial.reshape(YL * NX, YH * BLOCKS * 8, COLS)
    near = lax.all_to_all(sent, ("yl", "x"), 0, 0, tiled=True).sum(0)
    far = lax.all_to_all(near.reshape(YH, BLOCKS * 8, COLS), "yh", 0, 0, tiled=True)
    return final_rows(meta, far)


def solution(mesh):
    fine = Mesh(
        mesh.devices.reshape(YH, YL, NX, ZH, ZL, CORES), ("yh", "yl", "x", "zh", "zl", "c")
    )
    out = P(None, ("yh", "yl", "x"), ("zh", "zl", "c"))
    return jax.shard_map(
        per_device,
        mesh=fine,
        in_specs=(P(None, ("zl", "c"), ("yh", "yl", "x", "zh")), out, P(), P()),
        out_specs=out,
        check_vma=False,
    )
```

```python
import functools

import jax
import jax.numpy as jnp
from jax import lax
from jax.experimental import pallas as pl
from jax.experimental.pallas import tpu as pltpu
from jax.sharding import Mesh
from jax.sharding import PartitionSpec as P

NX, YH, YL, ZH, ZL, CORES = 4, 4, 2, 4, 4, 2
BLOCKS, ROWS, PAIRS, COLS = 5, 32, 96, 384
LANES = 128
PACKED = ROWS * PAIRS // LANES
HALF = ZL * ROWS
FULL = CORES * HALF
LIMIT = 24 * 1024 * 1024
COLUMN_LEFT, ROW_LEFT = BLOCKS + 1, 2 * BLOCKS + 1


def split(integrals_ref, bhi_ref, blo_ref):
    pad = jnp.zeros((LANES - PAIRS, COLS), jnp.bfloat16)
    for h in range(ZH):
        b = integrals_ref[0, h * PAIRS:(h + 1) * PAIRS, :]
        high = b.astype(jnp.bfloat16)
        low = (b - high.astype(jnp.float32)).astype(jnp.bfloat16)
        for ref, value in ((bhi_ref, high), (blo_ref, low)):
            ref[0, h * LANES:h * LANES + PAIRS, :] = value
            ref[0, h * LANES + PAIRS:(h + 1) * LANES, :] = pad


def split_integrals(integrals):
    halves = pl.BlockSpec((1, ZH * LANES, COLS), lambda g: (g, 0, 0))
    return pl.pallas_call(
        split,
        out_shape=[jax.ShapeDtypeStruct((BLOCKS, ZH * LANES, COLS), jnp.bfloat16)] * 2,
        grid=(BLOCKS,),
        in_specs=[pl.BlockSpec((1, COLS, COLS), lambda g: (g, 0, 0))],
        out_specs=[halves, halves],
        compiler_params=pltpu.CompilerParams(vmem_limit_bytes=LIMIT),
        cost_estimate=pl.CostEstimate(flops=5_000_000, bytes_accessed=7_000_000, transcendentals=0),
    )(integrals)


def pack(rows_ref, packed_ref):
    third = LANES - PAIRS
    rows = rows_ref[...]
    last = [rows[:, PACKED:, i * third:(i + 1) * third] for i in range(3)]
    packed_ref[:, :, :PAIRS] = rows[:, :PACKED]
    packed_ref[:, :, PAIRS:] = jnp.concatenate(last, axis=1)


def pack_rows(amplitudes):
    whole = pl.BlockSpec(memory_space=pltpu.VMEM)
    return pl.pallas_call(
        pack,
        out_shape=jax.ShapeDtypeStruct((BLOCKS, PACKED, LANES), jnp.float32),
        in_specs=[whole],
        out_specs=whole,
        compiler_params=pltpu.CompilerParams(vmem_limit_bytes=LIMIT),
    )(amplitudes)


def unpack(rows):
    last = [rows[i * 8:(i + 1) * 8, PAIRS:] for i in range(3)]
    return jnp.concatenate([rows[:, :PAIRS], jnp.concatenate(last, axis=1)], axis=0)


def product(meta_ref, own_ref, other_ref, bhi_ref, blo_ref, out_ref, ahi, alo):
    group = meta_ref[BLOCKS]
    for h in range(ZH):
        pad = slice(h * LANES + PAIRS, (h + 1) * LANES)
        for ref in (ahi, alo):
            ref[:, :, pad] = jnp.zeros((2, FULL, LANES - PAIRS), jnp.bfloat16)

    lane = lax.broadcasted_iota(jnp.int32, (ROWS, PAIRS), 1)
    dot = functools.partial(jnp.dot, preferred_element_type=jnp.float32)
    for g in range(BLOCKS):
        slot = g % 2
        left = meta_ref[g]
        for h in range(ZH):
            keep = lane < left - h * PAIRS
            at = slice(h * LANES, h * LANES + PAIRS)
            for l in range(ZL):
                z = h * ZL + l
                for part, ref in enumerate((own_ref, other_ref)):
                    down = group if part == 0 else 1 - group
                    a = unpack(ref[z + down * (ZH * ZL - 1 - 2 * z), g])
                    a = jnp.where(keep, a, 0.0)
                    high = a.astype(jnp.bfloat16)
                    rows = slice(part * HALF + l * ROWS, part * HALF + (l + 1) * ROWS)
                    ahi[slot, rows, at] = high
                    alo[slot, rows, at] = (a - high.astype(jnp.float32)).astype(jnp.bfloat16)
        total = dot(ahi[slot], bhi_ref[g]) + (dot(ahi[slot], blo_ref[g]) + dot(alo[slot], bhi_ref[g]))
        for part in range(CORES):
            for l in range(ZL):
                side = group if (l + part) % 2 == 0 else 1 - group
                for x in range(NX):
                    first = part * HALF + l * ROWS + x * 8
                    out_ref[side, x, l, g] = total[first:first + 8]


def partial_sums(meta, own, other, integrals):
    whole = pl.BlockSpec(memory_space=pltpu.VMEM)
    bhi, blo = split_integrals(integrals)
    return pl.pallas_call(
        product,
        out_shape=jax.ShapeDtypeStruct((YL, NX, YH, BLOCKS, 8, COLS), jnp.float32),
        in_specs=[pl.BlockSpec(memory_space=pltpu.SMEM)] + [whole] * 4,
        out_specs=whole,
        scratch_shapes=[pltpu.VMEM((2, FULL, ZH * LANES), jnp.bfloat16)] * 2,
        compiler_params=pltpu.CompilerParams(vmem_limit_bytes=LIMIT),
        cost_estimate=pl.CostEstimate(flops=1_200_000_000, bytes_accessed=8_000_000, transcendentals=0),
    )(meta, own, other, bhi, blo)


def finish(meta_ref, parts_ref, out_ref):
    row = lax.broadcasted_iota(jnp.int32, (8, COLS), 0)
    column = lax.broadcasted_iota(jnp.int32, (8, COLS), 1)
    for g in range(BLOCKS):
        rows = slice(g * 8, (g + 1) * 8)
        total = (parts_ref[0, rows] + parts_ref[1, rows]) + (parts_ref[2, rows] + parts_ref[3, rows])
        used = jnp.logical_and(row < meta_ref[ROW_LEFT + g], column < meta_ref[COLUMN_LEFT + g])
        out_ref[g] = jnp.where(used, total, 0.0)


def final_rows(meta, parts):
    whole = pl.BlockSpec(memory_space=pltpu.VMEM)
    return pl.pallas_call(
        finish,
        out_shape=jax.ShapeDtypeStruct((BLOCKS, 8, COLS), jnp.float32),
        in_specs=[pl.BlockSpec(memory_space=pltpu.SMEM), whole],
        out_specs=whole,
        compiler_params=pltpu.CompilerParams(vmem_limit_bytes=LIMIT),
    )(meta, parts)


def per_device(amplitudes, integrals, pair_counts, row_counts):
    y = lax.axis_index("yh") * YL + lax.axis_index("yl")
    gx = y * NX + lax.axis_index("x")
    core = lax.axis_index("c")
    group = lax.rem(core + lax.axis_index("zl"), CORES)
    column_first = ((lax.axis_index("zh") * ZL + lax.axis_index("zl")) * CORES + core) * COLS
    meta = jnp.concatenate(
        [pair_counts - gx * COLS, group[None], pair_counts - column_first, row_counts - gx * 8]
    )
    up = [z * CORES + z % CORES for z in range(ZH * ZL)]
    rings = [up, [device ^ 1 for device in reversed(up)]]
    own = lax.all_gather(pack_rows(amplitudes), ("zh", "zl", "c"), axis_index_groups=rings)
    other = lax.ppermute(own, "c", [(0, 1), (1, 0)])
    partial = partial_sums(meta, own, other, integrals)
    sent = partial.reshape(YL * NX, YH * BLOCKS * 8, COLS)
    near = lax.all_to_all(sent, ("yl", "x"), 0, 0, tiled=True).sum(0)
    far = lax.all_to_all(near.reshape(YH, BLOCKS * 8, COLS), "yh", 0, 0, tiled=True)
    return final_rows(meta, far)


def solution(mesh):
    fine = Mesh(
        mesh.devices.reshape(YH, YL, NX, ZH, ZL, CORES), ("yh", "yl", "x", "zh", "zl", "c")
    )
    out = P(None, ("yh", "yl", "x"), ("zh", "zl", "c"))
    return jax.shard_map(
        per_device,
        mesh=fine,
        in_specs=(P(None, ("zl", "c"), ("yh", "yl", "x", "zh")), out, P(), P()),
        out_specs=out,
        check_vma=False,
    )
```

```python
import functools

import jax
import jax.numpy as jnp
from jax import lax
from jax.experimental import pallas as pl
from jax.experimental.pallas import tpu as pltpu
from jax.sharding import Mesh
from jax.sharding import PartitionSpec as P

NX, YH, YL, ZH, ZL, CORES = 4, 4, 2, 4, 4, 2
BLOCKS, ROWS, PAIRS, COLS = 5, 32, 96, 384
LANES = 128
PACKED = ROWS * PAIRS // LANES
HALF = ZL * ROWS
FULL = CORES * HALF
LIMIT = 24 * 1024 * 1024
COLUMN_LEFT, ROW_LEFT = BLOCKS + 1, 2 * BLOCKS + 1


def split(integrals_ref, bhi_ref, blo_ref):
    pad = jnp.zeros((LANES - PAIRS, COLS), jnp.bfloat16)
    for h in range(ZH):
        b = integrals_ref[0, h * PAIRS:(h + 1) * PAIRS, :]
        high = b.astype(jnp.bfloat16)
        low = (b - high.astype(jnp.float32)).astype(jnp.bfloat16)
        for ref, value in ((bhi_ref, high), (blo_ref, low)):
            ref[0, h * LANES:h * LANES + PAIRS, :] = value
            ref[0, h * LANES + PAIRS:(h + 1) * LANES, :] = pad


def split_integrals(integrals):
    halves = pl.BlockSpec((1, ZH * LANES, COLS), lambda g: (g, 0, 0))
    return pl.pallas_call(
        split,
        out_shape=[jax.ShapeDtypeStruct((BLOCKS, ZH * LANES, COLS), jnp.bfloat16)] * 2,
        grid=(BLOCKS,),
        in_specs=[pl.BlockSpec((1, COLS, COLS), lambda g: (g, 0, 0))],
        out_specs=[halves, halves],
        compiler_params=pltpu.CompilerParams(vmem_limit_bytes=51000000),
        cost_estimate=pl.CostEstimate(flops=5_000_000, bytes_accessed=7_000_000, transcendentals=0),
    )(integrals)


def pack(rows_ref, packed_ref):
    third = LANES - PAIRS
    rows = rows_ref[...]
    last = [rows[:, PACKED:, i * third:(i + 1) * third] for i in range(3)]
    packed_ref[:, :, :PAIRS] = rows[:, :PACKED]
    packed_ref[:, :, PAIRS:] = jnp.concatenate(last, axis=1)


def pack_rows(amplitudes):
    whole = pl.BlockSpec(memory_space=pltpu.VMEM)
    return pl.pallas_call(
        pack,
        out_shape=jax.ShapeDtypeStruct((BLOCKS, PACKED, LANES), jnp.float32),
        in_specs=[whole],
        out_specs=whole,
        compiler_params=pltpu.CompilerParams(vmem_limit_bytes=LIMIT),
    )(amplitudes)


def unpack(rows):
    last = [rows[i * 8:(i + 1) * 8, PAIRS:] for i in range(3)]
    return jnp.concatenate([rows[:, :PAIRS], jnp.concatenate(last, axis=1)], axis=0)


def product(meta_ref, own_ref, other_ref, bhi_ref, blo_ref, out_ref, ahi, alo):
    group = meta_ref[BLOCKS]
    for h in range(ZH):
        pad = slice(h * LANES + PAIRS, (h + 1) * LANES)
        for ref in (ahi, alo):
            ref[:, :, pad] = jnp.zeros((2, FULL, LANES - PAIRS), jnp.bfloat16)

    lane = lax.broadcasted_iota(jnp.int32, (ROWS, PAIRS), 1)
    dot = functools.partial(jnp.dot, preferred_element_type=jnp.float32)
    for g in range(BLOCKS):
        slot = g % 2
        left = meta_ref[g]
        for h in range(ZH):
            keep = lane < left - h * PAIRS
            at = slice(h * LANES, h * LANES + PAIRS)
            for l in range(ZL):
                z = h * ZL + l
                for part, ref in enumerate((own_ref, other_ref)):
                    down = group if part == 0 else 1 - group
                    a = unpack(ref[z + down * (ZH * ZL - 1 - 2 * z), g])
                    a = jnp.where(keep, a, 0.0)
                    high = a.astype(jnp.bfloat16)
                    rows = slice(part * HALF + l * ROWS, part * HALF + (l + 1) * ROWS)
                    ahi[slot, rows, at] = high
                    alo[slot, rows, at] = (a - high.astype(jnp.float32)).astype(jnp.bfloat16)
        total = dot(ahi[slot], bhi_ref[g]) + (dot(ahi[slot], blo_ref[g]) + dot(alo[slot], bhi_ref[g]))
        for part in range(CORES):
            for l in range(ZL):
                side = group if (l + part) % 2 == 0 else 1 - group
                for x in range(NX):
                    first = part * HALF + l * ROWS + x * 8
                    out_ref[side, x, l, g] = total[first:first + 8]


def partial_sums(meta, own, other, integrals):
    whole = pl.BlockSpec(memory_space=pltpu.VMEM)
    bhi, blo = split_integrals(integrals)
    return pl.pallas_call(
        product,
        out_shape=jax.ShapeDtypeStruct((YL, NX, YH, BLOCKS, 8, COLS), jnp.float32),
        in_specs=[pl.BlockSpec(memory_space=pltpu.SMEM)] + [whole] * 4,
        out_specs=whole,
        scratch_shapes=[pltpu.VMEM((2, FULL, ZH * LANES), jnp.bfloat16)] * 2,
        compiler_params=pltpu.CompilerParams(vmem_limit_bytes=LIMIT),
        cost_estimate=pl.CostEstimate(flops=1_200_000_000, bytes_accessed=8_000_000, transcendentals=0),
    )(meta, own, other, bhi, blo)


def finish(meta_ref, parts_ref, out_ref):
    row = lax.broadcasted_iota(jnp.int32, (8, COLS), 0)
    column = lax.broadcasted_iota(jnp.int32, (8, COLS), 1)
    for g in range(BLOCKS):
        rows = slice(g * 8, (g + 1) * 8)
        total = (parts_ref[0, rows] + parts_ref[1, rows]) + (parts_ref[2, rows] + parts_ref[3, rows])
        used = jnp.logical_and(row < meta_ref[ROW_LEFT + g], column < meta_ref[COLUMN_LEFT + g])
        out_ref[g] = jnp.where(used, total, 0.0)


def final_rows(meta, parts):
    whole = pl.BlockSpec(memory_space=pltpu.VMEM)
    return pl.pallas_call(
        finish,
        out_shape=jax.ShapeDtypeStruct((BLOCKS, 8, COLS), jnp.float32),
        in_specs=[pl.BlockSpec(memory_space=pltpu.SMEM), whole],
        out_specs=whole,
        compiler_params=pltpu.CompilerParams(vmem_limit_bytes=LIMIT),
    )(meta, parts)


def per_device(amplitudes, integrals, pair_counts, row_counts):
    y = lax.axis_index("yh") * YL + lax.axis_index("yl")
    gx = y * NX + lax.axis_index("x")
    core = lax.axis_index("c")
    group = lax.rem(core + lax.axis_index("zl"), CORES)
    column_first = ((lax.axis_index("zh") * ZL + lax.axis_index("zl")) * CORES + core) * COLS
    meta = jnp.concatenate(
        [pair_counts - gx * COLS, group[None], pair_counts - column_first, row_counts - gx * 8]
    )
    up = [z * CORES + z % CORES for z in range(ZH * ZL)]
    rings = [up, [device ^ 1 for device in reversed(up)]]
    own = lax.all_gather(pack_rows(amplitudes), ("zh", "zl", "c"), axis_index_groups=rings)
    other = lax.ppermute(own, "c", [(0, 1), (1, 0)])
    partial = partial_sums(meta, own, other, integrals)
    sent = partial.reshape(YL * NX, YH * BLOCKS * 8, COLS)
    near = lax.all_to_all(sent, ("yl", "x"), 0, 0, tiled=True).sum(0)
    far = lax.all_to_all(near.reshape(YH, BLOCKS * 8, COLS), "yh", 0, 0, tiled=True)
    return final_rows(meta, far)


def solution(mesh):
    fine = Mesh(
        mesh.devices.reshape(YH, YL, NX, ZH, ZL, CORES), ("yh", "yl", "x", "zh", "zl", "c")
    )
    out = P(None, ("yh", "yl", "x"), ("zh", "zl", "c"))
    return jax.shard_map(
        per_device,
        mesh=fine,
        in_specs=(P(None, ("zl", "c"), ("yh", "yl", "x", "zh")), out, P(), P()),
        out_specs=out,
        check_vma=False,
    )
```

```python
import functools

import jax
import jax.numpy as jnp
from jax import lax
from jax.experimental import pallas as pl
from jax.experimental.pallas import tpu as pltpu
from jax.sharding import Mesh
from jax.sharding import PartitionSpec as P

NX, YH, YL, ZH, ZL, CORES = 4, 4, 2, 4, 4, 2
BLOCKS, ROWS, PAIRS, COLS = 5, 32, 96, 384
LANES = 128
PACKED = ROWS * PAIRS // LANES
HALF = ZL * ROWS
FULL = CORES * HALF
LIMIT = 24 * 1024 * 1024
COLUMN_LEFT, ROW_LEFT = BLOCKS + 1, 2 * BLOCKS + 1


def split(integrals_ref, bhi_ref, blo_ref, held, arrived):
    def fetch(g):
        return pltpu.make_async_copy(integrals_ref.at[g], held.at[g], arrived.at[g])

    for g in range(BLOCKS):
        fetch(g).start()
    pad = jnp.zeros((LANES - PAIRS, COLS), jnp.bfloat16)
    for g in range(BLOCKS):
        fetch(g).wait()
        for h in range(ZH):
            b = held[g, h * PAIRS:(h + 1) * PAIRS, :]
            high = b.astype(jnp.bfloat16)
            low = (b - high.astype(jnp.float32)).astype(jnp.bfloat16)
            for ref, value in ((bhi_ref, high), (blo_ref, low)):
                ref[g, h * LANES:h * LANES + PAIRS, :] = value
                ref[g, h * LANES + PAIRS:(h + 1) * LANES, :] = pad


def split_integrals(integrals):
    whole = pl.BlockSpec(memory_space=pltpu.VMEM)
    return pl.pallas_call(
        split,
        out_shape=[jax.ShapeDtypeStruct((BLOCKS, ZH * LANES, COLS), jnp.bfloat16)] * 2,
        in_specs=[pl.BlockSpec(memory_space=pltpu.HBM)],
        out_specs=[whole, whole],
        scratch_shapes=[
            pltpu.VMEM((BLOCKS, COLS, COLS), jnp.float32), pltpu.SemaphoreType.DMA((BLOCKS,))
        ],
        compiler_params=pltpu.CompilerParams(vmem_limit_bytes=51_000_000),
        cost_estimate=pl.CostEstimate(flops=5_000_000, bytes_accessed=7_000_000, transcendentals=0),
    )(integrals)


def pack(rows_ref, packed_ref):
    third = LANES - PAIRS
    rows = rows_ref[...]
    last = [rows[:, PACKED:, i * third:(i + 1) * third] for i in range(3)]
    packed_ref[:, :, :PAIRS] = rows[:, :PACKED]
    packed_ref[:, :, PAIRS:] = jnp.concatenate(last, axis=1)


def pack_rows(amplitudes):
    whole = pl.BlockSpec(memory_space=pltpu.VMEM)
    return pl.pallas_call(
        pack,
        out_shape=jax.ShapeDtypeStruct((BLOCKS, PACKED, LANES), jnp.float32),
        in_specs=[whole],
        out_specs=whole,
        compiler_params=pltpu.CompilerParams(vmem_limit_bytes=LIMIT),
    )(amplitudes)


def unpack(rows):
    last = [rows[i * 8:(i + 1) * 8, PAIRS:] for i in range(3)]
    return jnp.concatenate([rows[:, :PAIRS], jnp.concatenate(last, axis=1)], axis=0)


def product(meta_ref, own_ref, other_ref, bhi_ref, blo_ref, out_ref, ahi, alo):
    group = meta_ref[BLOCKS]
    for h in range(ZH):
        pad = slice(h * LANES + PAIRS, (h + 1) * LANES)
        for ref in (ahi, alo):
            ref[:, :, pad] = jnp.zeros((2, FULL, LANES - PAIRS), jnp.bfloat16)

    lane = lax.broadcasted_iota(jnp.int32, (ROWS, PAIRS), 1)
    dot = functools.partial(jnp.dot, preferred_element_type=jnp.float32)
    for g in range(BLOCKS):
        slot = g % 2
        left = meta_ref[g]
        for h in range(ZH):
            keep = lane < left - h * PAIRS
            at = slice(h * LANES, h * LANES + PAIRS)
            for l in range(ZL):
                z = h * ZL + l
                for part, ref in enumerate((own_ref, other_ref)):
                    down = group if part == 0 else 1 - group
                    a = unpack(ref[z + down * (ZH * ZL - 1 - 2 * z), g])
                    a = jnp.where(keep, a, 0.0)
                    high = a.astype(jnp.bfloat16)
                    rows = slice(part * HALF + l * ROWS, part * HALF + (l + 1) * ROWS)
                    ahi[slot, rows, at] = high
                    alo[slot, rows, at] = (a - high.astype(jnp.float32)).astype(jnp.bfloat16)
        total = dot(ahi[slot], bhi_ref[g]) + (dot(ahi[slot], blo_ref[g]) + dot(alo[slot], bhi_ref[g]))
        for part in range(CORES):
            for l in range(ZL):
                side = group if (l + part) % 2 == 0 else 1 - group
                for x in range(NX):
                    first = part * HALF + l * ROWS + x * 8
                    out_ref[side, x, l, g] = total[first:first + 8]


def partial_sums(meta, own, other, integrals):
    whole = pl.BlockSpec(memory_space=pltpu.VMEM)
    bhi, blo = split_integrals(integrals)
    return pl.pallas_call(
        product,
        out_shape=jax.ShapeDtypeStruct((YL, NX, YH, BLOCKS, 8, COLS), jnp.float32),
        in_specs=[pl.BlockSpec(memory_space=pltpu.SMEM)] + [whole] * 4,
        out_specs=whole,
        scratch_shapes=[pltpu.VMEM((2, FULL, ZH * LANES), jnp.bfloat16)] * 2,
        compiler_params=pltpu.CompilerParams(vmem_limit_bytes=LIMIT),
        cost_estimate=pl.CostEstimate(flops=1_200_000_000, bytes_accessed=8_000_000, transcendentals=0),
    )(meta, own, other, bhi, blo)


def finish(meta_ref, parts_ref, out_ref):
    row = lax.broadcasted_iota(jnp.int32, (8, COLS), 0)
    column = lax.broadcasted_iota(jnp.int32, (8, COLS), 1)
    for g in range(BLOCKS):
        rows = slice(g * 8, (g + 1) * 8)
        total = (parts_ref[0, rows] + parts_ref[1, rows]) + (parts_ref[2, rows] + parts_ref[3, rows])
        used = jnp.logical_and(row < meta_ref[ROW_LEFT + g], column < meta_ref[COLUMN_LEFT + g])
        out_ref[g] = jnp.where(used, total, 0.0)


def final_rows(meta, parts):
    whole = pl.BlockSpec(memory_space=pltpu.VMEM)
    return pl.pallas_call(
        finish,
        out_shape=jax.ShapeDtypeStruct((BLOCKS, 8, COLS), jnp.float32),
        in_specs=[pl.BlockSpec(memory_space=pltpu.SMEM), whole],
        out_specs=whole,
        compiler_params=pltpu.CompilerParams(vmem_limit_bytes=LIMIT),
    )(meta, parts)


def per_device(amplitudes, integrals, pair_counts, row_counts):
    y = lax.axis_index("yh") * YL + lax.axis_index("yl")
    gx = y * NX + lax.axis_index("x")
    core = lax.axis_index("c")
    group = lax.rem(core + lax.axis_index("zl"), CORES)
    column_first = ((lax.axis_index("zh") * ZL + lax.axis_index("zl")) * CORES + core) * COLS
    meta = jnp.concatenate(
        [pair_counts - gx * COLS, group[None], pair_counts - column_first, row_counts - gx * 8]
    )
    up = [z * CORES + z % CORES for z in range(ZH * ZL)]
    rings = [up, [device ^ 1 for device in reversed(up)]]
    own = lax.all_gather(pack_rows(amplitudes), ("zh", "zl", "c"), axis_index_groups=rings)
    other = lax.ppermute(own, "c", [(0, 1), (1, 0)])
    partial = partial_sums(meta, own, other, integrals)
    sent = partial.reshape(YL * NX, YH * BLOCKS * 8, COLS)
    near = lax.all_to_all(sent, ("yl", "x"), 0, 0, tiled=True).sum(0)
    far = lax.all_to_all(near.reshape(YH, BLOCKS * 8, COLS), "yh", 0, 0, tiled=True)
    return final_rows(meta, far)


def solution(mesh):
    fine = Mesh(
        mesh.devices.reshape(YH, YL, NX, ZH, ZL, CORES), ("yh", "yl", "x", "zh", "zl", "c")
    )
    out = P(None, ("yh", "yl", "x"), ("zh", "zl", "c"))
    return jax.shard_map(
        per_device,
        mesh=fine,
        in_specs=(P(None, ("zl", "c"), ("yh", "yl", "x", "zh")), out, P(), P()),
        out_specs=out,
        check_vma=False,
    )
```

```python
import functools

import jax
import jax.numpy as jnp
from jax import lax
from jax.experimental import pallas as pl
from jax.experimental.pallas import tpu as pltpu
from jax.sharding import Mesh
from jax.sharding import PartitionSpec as P

NX, YH, YL, ZH, ZL, CORES = 4, 4, 2, 4, 4, 2
BLOCKS, ROWS, PAIRS, COLS = 5, 32, 96, 384
LANES = 128
PACKED = ROWS * PAIRS // LANES
HALF = ZL * ROWS
FULL = CORES * HALF
SLOTS = 1
LIMIT = 24 * 1024 * 1024
COLUMN_LEFT, ROW_LEFT = BLOCKS + 1, 2 * BLOCKS + 1


def split(integrals_ref, bhi_ref, blo_ref, held, arrived):
    def fetch(g):
        return pltpu.make_async_copy(integrals_ref.at[g], held.at[g], arrived.at[g])

    for g in range(BLOCKS):
        fetch(g).start()
    pad = jnp.zeros((LANES - PAIRS, COLS), jnp.bfloat16)
    for g in range(BLOCKS):
        fetch(g).wait()
        for h in range(ZH):
            b = held[g, h * PAIRS:(h + 1) * PAIRS, :]
            high = b.astype(jnp.bfloat16)
            low = (b - high.astype(jnp.float32)).astype(jnp.bfloat16)
            for ref, value in ((bhi_ref, high), (blo_ref, low)):
                ref[g, h * LANES:h * LANES + PAIRS, :] = value
                ref[g, h * LANES + PAIRS:(h + 1) * LANES, :] = pad


def split_integrals(integrals):
    whole = pl.BlockSpec(memory_space=pltpu.VMEM)
    return pl.pallas_call(
        split,
        out_shape=[jax.ShapeDtypeStruct((BLOCKS, ZH * LANES, COLS), jnp.bfloat16)] * 2,
        in_specs=[pl.BlockSpec(memory_space=pltpu.HBM)],
        out_specs=[whole, whole],
        scratch_shapes=[
            pltpu.VMEM((BLOCKS, COLS, COLS), jnp.float32), pltpu.SemaphoreType.DMA((BLOCKS,))
        ],
        compiler_params=pltpu.CompilerParams(vmem_limit_bytes=51_000_000),
        cost_estimate=pl.CostEstimate(flops=5_000_000, bytes_accessed=7_000_000, transcendentals=0),
    )(integrals)


def pack(rows_ref, packed_ref):
    third = LANES - PAIRS
    rows = rows_ref[...]
    last = [rows[:, PACKED:, i * third:(i + 1) * third] for i in range(3)]
    packed_ref[:, :, :PAIRS] = rows[:, :PACKED]
    packed_ref[:, :, PAIRS:] = jnp.concatenate(last, axis=1)


def pack_rows(amplitudes):
    whole = pl.BlockSpec(memory_space=pltpu.VMEM)
    return pl.pallas_call(
        pack,
        out_shape=jax.ShapeDtypeStruct((BLOCKS, PACKED, LANES), jnp.float32),
        in_specs=[whole],
        out_specs=whole,
        compiler_params=pltpu.CompilerParams(vmem_limit_bytes=LIMIT),
    )(amplitudes)


def unpack(rows):
    last = [rows[i * 8:(i + 1) * 8, PAIRS:] for i in range(3)]
    return jnp.concatenate([rows[:, :PAIRS], jnp.concatenate(last, axis=1)], axis=0)


def product(meta_ref, own_ref, other_ref, bhi_ref, blo_ref, out_ref, ahi, alo):
    group = meta_ref[BLOCKS]
    for h in range(ZH):
        pad = slice(h * LANES + PAIRS, (h + 1) * LANES)
        for ref in (ahi, alo):
            ref[:, :, pad] = jnp.zeros((SLOTS, FULL, LANES - PAIRS), jnp.bfloat16)

    lane = lax.broadcasted_iota(jnp.int32, (ROWS, PAIRS), 1)
    dot = functools.partial(jnp.dot, preferred_element_type=jnp.float32)
    for g in range(BLOCKS):
        slot = g % SLOTS
        left = meta_ref[g]
        for h in range(ZH):
            keep = lane < left - h * PAIRS
            at = slice(h * LANES, h * LANES + PAIRS)
            for l in range(ZL):
                z = h * ZL + l
                for part, ref in enumerate((own_ref, other_ref)):
                    down = group if part == 0 else 1 - group
                    a = unpack(ref[z + down * (ZH * ZL - 1 - 2 * z), g])
                    a = jnp.where(keep, a, 0.0)
                    high = a.astype(jnp.bfloat16)
                    rows = slice(part * HALF + l * ROWS, part * HALF + (l + 1) * ROWS)
                    ahi[slot, rows, at] = high
                    alo[slot, rows, at] = (a - high.astype(jnp.float32)).astype(jnp.bfloat16)
        total = dot(ahi[slot], bhi_ref[g]) + (dot(ahi[slot], blo_ref[g]) + dot(alo[slot], bhi_ref[g]))
        for part in range(CORES):
            for l in range(ZL):
                side = group if (l + part) % 2 == 0 else 1 - group
                for x in range(NX):
                    first = part * HALF + l * ROWS + x * 8
                    out_ref[side, x, l, g] = total[first:first + 8]


def partial_sums(meta, own, other, integrals):
    whole = pl.BlockSpec(memory_space=pltpu.VMEM)
    bhi, blo = split_integrals(integrals)
    return pl.pallas_call(
        product,
        out_shape=jax.ShapeDtypeStruct((YL, NX, YH, BLOCKS, 8, COLS), jnp.float32),
        in_specs=[pl.BlockSpec(memory_space=pltpu.SMEM)] + [whole] * 4,
        out_specs=whole,
        scratch_shapes=[pltpu.VMEM((SLOTS, FULL, ZH * LANES), jnp.bfloat16)] * 2,
        compiler_params=pltpu.CompilerParams(vmem_limit_bytes=LIMIT),
        cost_estimate=pl.CostEstimate(flops=1_200_000_000, bytes_accessed=8_000_000, transcendentals=0),
    )(meta, own, other, bhi, blo)


def finish(meta_ref, parts_ref, out_ref):
    row = lax.broadcasted_iota(jnp.int32, (8, COLS), 0)
    column = lax.broadcasted_iota(jnp.int32, (8, COLS), 1)
    for g in range(BLOCKS):
        rows = slice(g * 8, (g + 1) * 8)
        total = (parts_ref[0, rows] + parts_ref[1, rows]) + (parts_ref[2, rows] + parts_ref[3, rows])
        used = jnp.logical_and(row < meta_ref[ROW_LEFT + g], column < meta_ref[COLUMN_LEFT + g])
        out_ref[g] = jnp.where(used, total, 0.0)


def final_rows(meta, parts):
    whole = pl.BlockSpec(memory_space=pltpu.VMEM)
    return pl.pallas_call(
        finish,
        out_shape=jax.ShapeDtypeStruct((BLOCKS, 8, COLS), jnp.float32),
        in_specs=[pl.BlockSpec(memory_space=pltpu.SMEM), whole],
        out_specs=whole,
        compiler_params=pltpu.CompilerParams(vmem_limit_bytes=LIMIT),
    )(meta, parts)


def per_device(amplitudes, integrals, pair_counts, row_counts):
    y = lax.axis_index("yh") * YL + lax.axis_index("yl")
    gx = y * NX + lax.axis_index("x")
    core = lax.axis_index("c")
    group = lax.rem(core + lax.axis_index("zl"), CORES)
    column_first = ((lax.axis_index("zh") * ZL + lax.axis_index("zl")) * CORES + core) * COLS
    meta = jnp.concatenate(
        [pair_counts - gx * COLS, group[None], pair_counts - column_first, row_counts - gx * 8]
    )
    up = [z * CORES + z % CORES for z in range(ZH * ZL)]
    rings = [up, [device ^ 1 for device in reversed(up)]]
    own = lax.all_gather(pack_rows(amplitudes), ("zh", "zl", "c"), axis_index_groups=rings)
    other = lax.ppermute(own, "c", [(0, 1), (1, 0)])
    partial = partial_sums(meta, own, other, integrals)
    sent = partial.reshape(YL * NX, YH * BLOCKS * 8, COLS)
    near = lax.all_to_all(sent, ("yl", "x"), 0, 0, tiled=True).sum(0)
    far = lax.all_to_all(near.reshape(YH, BLOCKS * 8, COLS), "yh", 0, 0, tiled=True)
    return final_rows(meta, far)


def solution(mesh):
    fine = Mesh(
        mesh.devices.reshape(YH, YL, NX, ZH, ZL, CORES), ("yh", "yl", "x", "zh", "zl", "c")
    )
    out = P(None, ("yh", "yl", "x"), ("zh", "zl", "c"))
    return jax.shard_map(
        per_device,
        mesh=fine,
        in_specs=(P(None, ("zl", "c"), ("yh", "yl", "x", "zh")), out, P(), P()),
        out_specs=out,
        check_vma=False,
    )
```
